512 devices in a mesh: tiles: 128 (over y, z, core), pairs: 4 (over x).
Axes of the slice: x: 4, y: 8, z: 8, core: 2. Of those that a mesh axis runs over, the one named last changes fastest.
Arguments:
- amplitudes: bfloat16 [32, 16384], P(None, 'tiles'), may hold values from -6 to 6
- integrals: bfloat16 [128, 4, 96, 128, 128], P('tiles', 'pairs'), may hold values from -0.02734375 to 0.02734375
- block_owner: int32 [128, 4, 96, 1], P('tiles', 'pairs'), may hold values from 0 to 127; in each aligned block of 96 rows (0 to 95, 96 to 191, ..., all dimensions but the last counted through in order) no two rows name the same one
- tile_dims: int32 [128], P('tiles'), may hold values from 1 to 128, as said below
- energy_gap: float32 [32, 16384], P('pairs', 'tiles'), may hold values from 0.5 to 4
Outputs:
- residual: float32 [32, 16384], P('pairs', 'tiles')
- updated: bfloat16 [32, 16384], P('pairs', 'tiles')
The draws below stay inside these ranges and needn't reach their ends.
Inputs may be any that keep to these rules, and one draw needn't show every extreme that they name: `block_owner`: within one tile's list in one sub-slice the 96 named tiles are distinct. `tile_dims`: columns of a tile at or beyond its entry are padding; some tile is full.
All inputs are finite; a program needn't handle non-finite values.
Results may differ from the reference program's by a relative error of at most 0.0095.
Values may be sent and summed in bfloat16 or wider, within the bound.
A program may use at most 64 MiB of HBM per device.

```python
import math
import jax
import jax.numpy as jnp
import numpy as np
from jax import lax

W = 128
ROWS = 32
NT = 128
LP = 96
N_PAIRS = 4


def draw_tile_dims(key, part):
    key = jax.random.fold_in(key, 11)
    dims_key, full_key = jax.random.split(key)
    live_dims = jax.random.randint(dims_key, (NT,), 1, W + 1)
    full_tile = jax.random.randint(full_key, (), 0, NT)
    return jnp.where(jnp.arange(NT) == full_tile, W, live_dims).astype(jnp.int32)


def steps_of(rng, dims, cuts, low, top_value):
    level, own = 1.0, jax.random.fold_in(rng, 6)
    for position, blocks in cuts:
        heights = jnp.exp(jax.random.uniform(jax.random.fold_in(own, position), (blocks,), jnp.float32, low / len(cuts), top_value / len(cuts)))
        level = level * jnp.repeat(heights, dims[position] // blocks).reshape([-1 if axis == position else 1 for axis in range(len(dims))])
    return level


def shared_out(stream_key, own, number, rows, number_of, top, reach, skew):
    order = jax.random.permutation(stream_key, number_of)
    crowded, usual = shares(number_of, rows * top, reach, skew, True), shares(number_of, rows * top, reach, skew, False)
    places = jnp.arange(number_of)

    def named(lengths, offset_by):
        used = int((lengths > 0).sum())
        fixed = max(1, used // 4)
        passed = fixed + (places - fixed + offset_by * (used - fixed)) % max(1, number_of - fixed)
        return jnp.zeros((number_of,), jnp.int32).at[order[jnp.where(places < fixed, places, passed)]].set(jnp.asarray(lengths, jnp.int32))

    lengths = jnp.where(number % 4 == 0, named(crowded, number // 4), named(usual, number - number // 4 - 1))
    mixed = jax.random.permutation(jax.random.fold_in(own, 3), number_of)
    source_of, sink = mixed[0:number_of // 2 * 2:2], mixed[1:number_of // 2 * 2:2]
    slack = jnp.minimum(lengths[source_of] - 1, reach - lengths[sink]) // 2
    slack = jnp.where((source_of == order[0]) | (sink == order[0]) | (lengths[sink] == 0), 0, jnp.maximum(slack, 0))
    passed = jax.random.randint(jax.random.fold_in(own, 4), (number_of // 2,), 0, 1 << 20) % (slack + 1)
    lengths = lengths.at[source_of].add(-passed).at[sink].add(passed)
    labels = jnp.searchsorted(jnp.cumsum(lengths), jnp.arange(rows * top), side="right").astype(jnp.int32)
    listing = labels.reshape(top, rows).T
    listing = listing[jax.random.permutation(jax.random.fold_in(own, 1), rows)]
    offset_by = jax.random.randint(jax.random.fold_in(own, 2), (rows, 1), 0, top)
    return jnp.take_along_axis(listing, (jnp.arange(top)[None, :] + offset_by) % top, axis=1)


def shares(amount, total, most, slope, full):
    portions = [(1 << 20) // math.isqrt(rank ** slope) + 1 for rank in range(1, amount + 1)]
    largest = most if full else min(most, max(-(-total // amount), total * portions[0] // sum(portions)))
    least = 1 if total - largest >= amount - 1 else 0
    given, surplus = [largest] + [least] * (amount - 1), total - largest - least * (amount - 1)
    while surplus > 0:
        movable = [i for i in range(1, amount) if given[i] < largest] or [i for i in range(1, amount) if given[i] < most]
        whole, remaining = sum([portions[i] for i in movable]), surplus
        for i in movable:
            more = min(most - given[i], max(1, remaining * portions[i] // whole), surplus)
            given[i] = given[i] + more
            surplus = surplus - more
    return np.array(given)


def scatter_about(own_key, extent, width, most, pieces=(), kind=jnp.bfloat16):
    drawn = width * jax.random.normal(own_key, extent, jnp.float32)
    if pieces:
        drawn = drawn * steps_of(own_key, extent, pieces, -0.22, 0.18)
    return jnp.clip(drawn, -most, most).astype(kind)


def setup_inputs(seed: int = 0) -> dict:
    key_of = jax.random.split(jax.random.key(seed), 6)
    amplitudes = scatter_about(key_of[0], (ROWS, NT * W), 1.0, 6.0, ((1, 128),))
    integrals = scatter_about(key_of[1], (NT, N_PAIRS, LP, W, W), (W * LP * N_PAIRS) ** -0.5, 0.02734375, ((0, 128), (1, 4)))
    block_owner_keys = jax.random.split(jax.random.fold_in(key_of[2], 1), NT * N_PAIRS * LP // LP)
    block_owner_turns = jax.random.permutation(jax.random.fold_in(key_of[2], 3), NT * N_PAIRS * LP // LP)
    block_owner = jax.vmap(lambda own, number: shared_out(jax.random.fold_in(key_of[2], 2), own, number, LP, NT, 1, 1, 2))(block_owner_keys, block_owner_turns).reshape((NT, N_PAIRS, LP, 1))
    tile_dims = draw_tile_dims(jax.random.fold_in(key_of[5], 71), 0)
    energy_gap = jnp.clip(jnp.exp(math.log(4.0) - 2.0794415 * jax.random.uniform(key_of[4], (ROWS, NT * W), jnp.float32) ** steps_of(key_of[4], (ROWS, NT * W), ((0, 4), (1, 128)), -0.2, 0.2)), 0.5, 4.0)
    return dict(amplitudes=amplitudes, integrals=integrals, block_owner=block_owner, tile_dims=tile_dims, energy_gap=energy_gap)


def reference(amplitudes, integrals, block_owner, tile_dims, energy_gap):
    row_count = amplitudes.shape[0]
    tile_number = tile_dims.shape[0]
    tile_width = integrals.shape[-1]
    columns = jnp.arange(tile_width, dtype=jnp.int32)
    live_mask = columns[None, :] < tile_dims[:, None]
    live_flat = live_mask.reshape(1, tile_number * tile_width)
    masked = jnp.where(live_flat, amplitudes, jnp.zeros_like(amplitudes))
    tiles_view = masked.reshape(row_count, tile_number, tile_width)

    def one_tile(members):
        blocks, owners = members
        flat_blocks = blocks.reshape(-1, tile_width, tile_width).astype(jnp.float32)
        flat_owners = owners.reshape(-1).astype(jnp.int32)
        chosen = jnp.take(tiles_view, flat_owners, axis=1).astype(jnp.float32)
        products = jnp.einsum("rsc,skc->srk", chosen, flat_blocks).astype(jnp.bfloat16)
        return jnp.sum(products.astype(jnp.float32), axis=0)

    tile_sums = lax.map(one_tile, (integrals, block_owner))
    residual = jnp.transpose(tile_sums, (1, 0, 2)).reshape(row_count, tile_number * tile_width)
    residual = jnp.where(live_flat, residual, jnp.zeros_like(residual))
    updated = (masked.astype(jnp.float32) - residual / energy_gap).astype(jnp.bfloat16)
    return residual, updated
```

```python
import jax
import jax.numpy as jnp
from jax import lax
from jax.experimental import pallas as pl
from jax.experimental.pallas import tpu as pltpu
from jax.sharding import PartitionSpec as P

RING = 8
HALF = RING // 2
GROUP = 2
GROUPS = HALF // GROUP
CHUNKS = 4
STEPS = (4, 3, 5, 2, 6, 1, 7)
NT_DIMS = (((1,), (1,)), ((), ()))


def kernel(
    owners_in,
    dims_in,
    amplitudes,
    integrals,
    energy_gap,
    out,
    owners,
    dims,
    raw,
    gap,
    blocks,
    mine,
    mine_wide,
    gathered,
    entry_rows,
    entries,
    terms,
    arrived,
    load_sems,
    entry_sems,
    partner_send,
    partner_recv,
    first_send,
    first_recv,
    second_send,
    second_recv,
    sum_send,
    sum_recv,
):
    tile = lax.axis_index("tiles")
    pair = lax.axis_index("pairs")
    pairs = lax.axis_size("pairs")
    core = tile % 2
    z = (tile // 2) % RING
    y = tile // (2 * RING)
    kind = (y + z) % 2
    partner = tile + 1 - 2 * core
    count = blocks.shape[1] - 1
    part = count // CHUNKS

    def along_z(step):
        return (y * RING + (z + step) % RING) * 2 + core

    def along_y(step):
        return (((y + step) % RING) * RING + z) * 2 + core

    load_raw = pltpu.make_async_copy(amplitudes, raw, load_sems.at[0])
    load_dims = pltpu.make_async_copy(dims_in, dims, load_sems.at[1])
    load_owners = pltpu.make_async_copy(owners_in, owners, load_sems.at[2])
    load_gap = pltpu.make_async_copy(energy_gap, gap, load_sems.at[3])
    load_raw.start()
    load_dims.start()

    barrier = pltpu.get_barrier_semaphore()
    for step in STEPS:
        pl.semaphore_signal(barrier, inc=1, device_id={"tiles": along_z(step)})
        pl.semaphore_signal(barrier, inc=1, device_id={"tiles": along_y(step)})
    for step in range(1, pairs):
        other = (pair + step) % pairs
        pl.semaphore_signal(barrier, inc=1, device_id={"pairs": other})
        pl.semaphore_signal(barrier, inc=1, device_id={"tiles": partner, "pairs": other})
    pl.semaphore_signal(barrier, inc=1, device_id={"tiles": partner})

    load_owners.start()
    load_gap.start()
    load_blocks = []
    for i in range(CHUNKS):
        rows = pl.ds(i * part, part)
        load = pltpu.make_async_copy(
            integrals.at[0, 0, rows], blocks.at[0, rows], load_sems.at[4 + i]
        )
        load.start()
        load_blocks.append(load)
    blocks[0, count] = jnp.zeros(blocks.shape[2:], blocks.dtype)
    blocks[1, count] = jnp.zeros(blocks.shape[2:], blocks.dtype)

    load_dims.wait()
    load_raw.wait()
    columns = lax.broadcasted_iota(jnp.int32, raw.shape, 1)
    masked = jnp.where(columns < dims[0], raw[...].astype(jnp.float32), 0.0)
    mine[...] = masked.astype(jnp.bfloat16)
    own_rows = gap.shape[0]
    for group in range(pairs):
        mine_wide[group] = masked[group * own_rows : (group + 1) * own_rows]
    major = jnp.where(kind == 0, y, z)
    minor = jnp.where(kind == 0, z, y) // 2
    slot = gathered.at[kind, major, minor]
    keep = pltpu.make_async_copy(mine, slot, first_recv.at[kind, minor // GROUP])
    keep.start()

    pl.semaphore_wait(barrier, 2 * (RING - 1) + 2 * (pairs - 1) + 1)

    first = []
    for step in STEPS:
        copy = pltpu.make_async_remote_copy(
            src_ref=mine,
            dst_ref=slot,
            send_sem=first_send.at[step - 1],
            recv_sem=first_recv.at[kind, minor // GROUP],
            device_id={"tiles": jnp.where(kind == 0, along_z(step), along_y(step))},
        )
        copy.start()
        first.append(copy)

    partner_copies = []
    for i in range(CHUNKS):
        rows = pl.ds(i * part, part)
        copy = pltpu.make_async_remote_copy(
            src_ref=integrals.at[0, 0, rows],
            dst_ref=blocks.at[1, rows],
            send_sem=partner_send.at[i],
            recv_sem=partner_recv.at[i],
            device_id={"tiles": partner},
        )
        copy.start()
        partner_copies.append(copy)

    load_owners.wait()
    width = raw.shape[1]
    row = jnp.broadcast_to(owners[...], (width, count))
    row = jnp.concatenate([row, jnp.full((width, width - count), -1, jnp.int32)], axis=1)
    named = row.T == lax.broadcasted_iota(jnp.int32, (width, width), 1)
    places = lax.broadcasted_iota(jnp.int32, (width, width), 0)
    place = jnp.min(jnp.where(named, places, count), axis=0, keepdims=True)
    entry_rows[0] = jnp.broadcast_to(place, entry_rows.shape[1:])
    copy = pltpu.make_async_remote_copy(
        src_ref=entry_rows.at[0],
        dst_ref=entry_rows.at[1],
        send_sem=partner_send.at[CHUNKS],
        recv_sem=partner_recv.at[CHUNKS],
        device_id={"tiles": partner},
    )
    copy.start()
    partner_copies.append(copy)
    own_entries = pltpu.make_async_copy(entry_rows.at[0], entries.at[0], entry_sems.at[0])
    own_entries.start()

    second = {}
    for group in range(GROUPS):
        for which in range(2):
            ref = gathered.at[which, 0, pl.ds(0, GROUP)]
            pltpu.make_async_copy(ref, ref, first_recv.at[which, group]).wait()
        for step in STEPS:
            for which in range(2):
                line = y if which == 0 else z
                ref = gathered.at[which, line, pl.ds(group * GROUP, GROUP)]
                copy = pltpu.make_async_remote_copy(
                    src_ref=ref,
                    dst_ref=ref,
                    send_sem=second_send.at[which, group, step - 1],
                    recv_sem=second_recv.at[which, group, step - 1],
                    device_id={"tiles": along_y(step) if which == 0 else along_z(step)},
                )
                copy.start()
                second[which, group, step] = copy

    for load in load_blocks:
        load.wait()
    partner_copies[CHUNKS].wait_recv()
    their_entries = pltpu.make_async_copy(entry_rows.at[1], entries.at[1], entry_sems.at[1])
    their_entries.start()
    for copy in partner_copies[:CHUNKS]:
        copy.wait_recv()
    own_entries.wait()
    their_entries.wait()

    def product(which, line, index):
        low = 2 * index + (line + which) % 2
        source = (line * RING + low if which == 0 else low * RING + line) * 2 + core
        listed = [blocks[which_list, entries[which_list, 0, source]] for which_list in range(2)]
        return gathered[which, line, index], jnp.concatenate(listed, axis=0)

    total = jnp.zeros((raw.shape[0], 2 * width), jnp.float32)

    def add_line(total, which, line, group):
        pieces = [product(which, line, group * GROUP + i) for i in range(GROUP)]
        left = jnp.concatenate([piece[0] for piece in pieces], axis=1)
        right = jnp.concatenate([piece[1] for piece in pieces], axis=1)
        return total + lax.dot_general(left, right, NT_DIMS, preferred_element_type=jnp.float32)

    for group in range(GROUPS):
        for which in range(2):
            total = add_line(total, which, y if which == 0 else z, group)
        for step in reversed(STEPS):
            for which in range(2):
                second[which, group, step].wait_recv()
                line = ((y if which == 0 else z) + RING - step) % RING
                total = add_line(total, which, line, group)
    for which_list in range(2):
        for group in range(pairs):
            terms[which_list, group] = total[
                group * own_rows : (group + 1) * own_rows,
                which_list * width : (which_list + 1) * width,
            ]

    sums = []
    for step in (2, 1, 3, 0):
        other = (pair + step) % pairs
        for which_list in (1, 0):
            if step == 0 and which_list == 0:
                continue
            number = which_list * pairs + step - 1
            copy = pltpu.make_async_remote_copy(
                src_ref=terms.at[which_list, other],
                dst_ref=arrived.at[number],
                send_sem=sum_send.at[number],
                recv_sem=sum_recv.at[number],
                device_id={"tiles": partner if which_list else tile, "pairs": other},
            )
            copy.start()
            sums.append(copy)
    load_gap.wait()
    keep_sends = first + list(second.values()) + partner_copies
    for copy in keep_sends:
        copy.wait_send()
    for copy in sums:
        copy.wait_recv()
    summed = terms[0, pair]
    for number in range(2 * pairs - 1):
        summed += arrived[number]
    live = lax.broadcasted_iota(jnp.int32, summed.shape, 1) < dims[0]
    summed = jnp.where(live, summed, 0.0)
    out[:own_rows] = summed
    out[own_rows:] = mine_wide[pair] - summed / gap[...]
    for copy in sums:
        copy.wait_send()


def per_device(amplitudes, integrals, block_owner, tile_dims, energy_gap):
    rows, width = amplitudes.shape
    count = integrals.shape[2]
    own_rows = energy_gap.shape[0]
    pairs = rows // own_rows
    dma = pltpu.SemaphoreType.DMA
    out = pl.pallas_call(
        kernel,
        out_shape=jax.ShapeDtypeStruct((2 * own_rows, width), jnp.float32),
        in_specs=[pl.BlockSpec(memory_space=pltpu.HBM)] * 5,
        out_specs=pl.BlockSpec(memory_space=pltpu.VMEM),
        scratch_shapes=[
            pltpu.VMEM((1, count), jnp.int32),
            pltpu.SMEM((1,), jnp.int32),
            pltpu.VMEM((rows, width), jnp.bfloat16),
            pltpu.VMEM((own_rows, width), jnp.float32),
            pltpu.VMEM((2, count + 1, width, width), jnp.bfloat16),
            pltpu.VMEM((rows, width), jnp.bfloat16),
            pltpu.VMEM((pairs, own_rows, width), jnp.float32),
            pltpu.VMEM((2, RING, HALF, rows, width), jnp.bfloat16),
            pltpu.VMEM((2, 8, width), jnp.int32),
            pltpu.SMEM((2, 8, width), jnp.int32),
            pltpu.VMEM((2, pairs, own_rows, width), jnp.float32),
            pltpu.VMEM((2 * pairs - 1, own_rows, width), jnp.float32),
            dma((4 + CHUNKS,)),
            dma((2,)),
            dma((CHUNKS + 1,)),
            dma((CHUNKS + 1,)),
            dma((RING - 1,)),
            dma((2, GROUPS)),
            dma((2, GROUPS, RING - 1)),
            dma((2, GROUPS, RING - 1)),
            dma((2 * pairs - 1,)),
            dma((2 * pairs - 1,)),
        ],
        compiler_params=pltpu.CompilerParams(
            collective_id=0, has_side_effects=True, vmem_limit_bytes=62 * 2**20
        ),
        cost_estimate=pl.CostEstimate(
            flops=2 * count * rows * width * width,
            bytes_accessed=2 * count * width * width,
            transcendentals=0,
        ),
    )(block_owner.reshape(1, count), tile_dims, amplitudes, integrals, energy_gap)
    return out[:own_rows], out[own_rows:].astype(jnp.bfloat16)


def solution(mesh):
    in_specs = (
        P(None, "tiles"),
        P("tiles", "pairs", None, None, None),
        P("tiles", "pairs", None, None),
        P("tiles"),
        P("pairs", "tiles"),
    )
    out_specs = (P("pairs", "tiles"), P("pairs", "tiles"))
    return jax.shard_map(
        per_device, mesh=mesh, in_specs=in_specs, out_specs=out_specs, check_vma=False
    )
```

```python
import jax
import jax.numpy as jnp
from jax import lax
from jax.experimental import pallas as pl
from jax.experimental.pallas import tpu as pltpu
from jax.sharding import PartitionSpec as P

RING = 8
HALF = RING // 2
GROUP = 2
GROUPS = HALF // GROUP
CHUNKS = 4
STEPS = (4, 3, 5, 2, 6, 1, 7)
EARLY, LATE = range(HALF), range(HALF, RING)
NT_DIMS = (((1,), (1,)), ((), ()))


def kernel(
    owners_in,
    dims_in,
    amplitudes,
    integrals,
    out,
    owners,
    dims,
    raw,
    blocks,
    mine,
    mine_wide,
    gathered,
    entry_rows,
    entries,
    terms,
    arrived,
    load_sems,
    entry_sems,
    partner_send,
    partner_recv,
    late_in,
    late_go,
    row_send,
    column_send,
    first_recv,
    row_line_send,
    column_line_send,
    second_recv,
    sum_send,
    sum_recv,
):
    tile = lax.axis_index("tiles")
    pair = lax.axis_index("pairs")
    pairs = lax.axis_size("pairs")
    core = tile % 2
    z = (tile // 2) % RING
    y = tile // (2 * RING)
    kind = (y + z) % 2
    partner = tile + 1 - 2 * core
    count = blocks.shape[1] - 1
    part = count // CHUNKS

    early = z < HALF

    def in_row(column):
        return (y * RING + column) * 2 + core

    def along_y(step):
        return (((y + step) % RING) * RING + z) * 2 + core

    load_raw = pltpu.make_async_copy(amplitudes, raw, load_sems.at[0])
    load_dims = pltpu.make_async_copy(dims_in, dims, load_sems.at[1])
    load_owners = pltpu.make_async_copy(owners_in, owners, load_sems.at[2])
    load_raw.start()
    load_dims.start()

    barrier = pltpu.get_barrier_semaphore()
    for step in STEPS:
        pl.semaphore_signal(barrier, inc=1, device_id={"tiles": along_y(step)})
    for step in range(1, pairs):
        other = (pair + step) % pairs
        pl.semaphore_signal(barrier, inc=1, device_id={"pairs": other})
        pl.semaphore_signal(barrier, inc=1, device_id={"tiles": partner, "pairs": other})
    pl.semaphore_signal(barrier, inc=1, device_id={"tiles": partner})

    @pl.when(early)
    def _():
        for step in STEPS:
            pl.semaphore_signal(barrier, inc=1, device_id={"tiles": in_row((z + step) % RING)})

    load_owners.start()
    load_blocks = []
    for i in range(CHUNKS):
        rows = pl.ds(i * part, part)
        load = pltpu.make_async_copy(
            integrals.at[0, 0, rows], blocks.at[0, rows], load_sems.at[3 + i]
        )
        load.start()
        load_blocks.append(load)
    blocks[0, count] = jnp.zeros(blocks.shape[2:], blocks.dtype)
    blocks[1, count] = jnp.zeros(blocks.shape[2:], blocks.dtype)

    load_dims.wait()
    load_raw.wait()
    columns = lax.broadcasted_iota(jnp.int32, raw.shape, 1)
    masked = jnp.where(columns < dims[0], raw[...].astype(jnp.float32), 0.0)
    mine[...] = masked.astype(jnp.bfloat16)
    own_rows = terms.shape[2]
    for group in range(pairs):
        mine_wide[group] = masked[group * own_rows : (group + 1) * own_rows]
    major = jnp.where(kind == 0, y, z)
    minor = jnp.where(kind == 0, z, y) // 2
    slot = gathered.at[kind, major, minor]
    keep = pltpu.make_async_copy(mine, slot, first_recv.at[kind, minor // GROUP])
    keep.start()

    from_row = jnp.where(early, HALF - 1, HALF)
    pl.semaphore_wait(barrier, RING - 1 + 2 * (pairs - 1) + 1 + from_row)

    row_copies = []
    for column in range(RING):
        copy = pltpu.make_async_remote_copy(
            src_ref=mine,
            dst_ref=slot,
            send_sem=row_send.at[column],
            recv_sem=first_recv.at[0, minor // GROUP],
            device_id={"tiles": in_row(column)},
        )
        row_copies.append((jnp.logical_and(kind == 0, z != column), copy))
    column_copies = []
    for step in STEPS:
        copy = pltpu.make_async_remote_copy(
            src_ref=mine,
            dst_ref=slot,
            send_sem=column_send.at[step - 1],
            recv_sem=first_recv.at[1, minor // GROUP],
            device_id={"tiles": along_y(step)},
        )
        column_copies.append((kind == 1, copy))
    for column in EARLY:
        pl.when(row_copies[column][0])(row_copies[column][1].start)

    @pl.when(kind == 1)
    def _():
        for _, copy in column_copies:
            copy.start()

    @pl.when(jnp.logical_not(early))
    def _():
        for column in EARLY:
            pl.semaphore_signal(late_in, inc=1, device_id={"tiles": in_row(column)})

    partner_copies = []
    for i in range(CHUNKS):
        rows = pl.ds(i * part, part)
        copy = pltpu.make_async_remote_copy(
            src_ref=integrals.at[0, 0, rows],
            dst_ref=blocks.at[1, rows],
            send_sem=partner_send.at[i],
            recv_sem=partner_recv.at[i],
            device_id={"tiles": partner},
        )
        copy.start()
        partner_copies.append(copy)

    load_owners.wait()
    width = raw.shape[1]
    row = jnp.broadcast_to(owners[...], (width, count))
    row = jnp.concatenate([row, jnp.full((width, width - count), -1, jnp.int32)], axis=1)
    named = row.T == lax.broadcasted_iota(jnp.int32, (width, width), 1)
    places = lax.broadcasted_iota(jnp.int32, (width, width), 0)
    place = jnp.min(jnp.where(named, places, count), axis=0, keepdims=True)
    entry_rows[0] = jnp.broadcast_to(place, entry_rows.shape[1:])
    copy = pltpu.make_async_remote_copy(
        src_ref=entry_rows.at[0],
        dst_ref=entry_rows.at[1],
        send_sem=partner_send.at[CHUNKS],
        recv_sem=partner_recv.at[CHUNKS],
        device_id={"tiles": partner},
    )
    copy.start()
    partner_copies.append(copy)
    own_entries = pltpu.make_async_copy(entry_rows.at[0], entries.at[0], entry_sems.at[0])
    own_entries.start()

    def wait_first(which, group):
        ref = gathered.at[which, 0, pl.ds(0, GROUP)]
        pltpu.make_async_copy(ref, ref, first_recv.at[which, group]).wait()

    row_lines = {}
    for group in range(GROUPS):
        for column in range(RING):
            ref = gathered.at[1, z, pl.ds(group * GROUP, GROUP)]
            copy = pltpu.make_async_remote_copy(
                src_ref=ref,
                dst_ref=ref,
                send_sem=row_line_send.at[group, column],
                recv_sem=second_recv.at[1, group, (column + RING - 1 - z) % RING],
                device_id={"tiles": in_row(column)},
            )
            row_lines[group, column] = (z != column, copy)
    def send_early_lines():
        for group in range(GROUPS):
            wait_first(1, group)
            for column in EARLY:
                pl.when(row_lines[group, column][0])(row_lines[group, column][1].start)

    @pl.when(early)
    def _():
        send_early_lines()
        pl.semaphore_wait(late_in, HALF)

    @pl.when(z == 0)
    def _():
        for column in LATE:
            pl.semaphore_signal(late_go, inc=1, device_id={"tiles": in_row(column)})

    @pl.when(jnp.logical_not(early))
    def _():
        send_early_lines()
        pl.semaphore_wait(late_go, 1)

    for column in LATE:
        pl.when(row_copies[column][0])(row_copies[column][1].start)
    for group in range(GROUPS):
        for column in LATE:
            pl.when(row_lines[group, column][0])(row_lines[group, column][1].start)
    column_lines = {}
    for group in range(GROUPS):
        wait_first(0, group)
        for step in STEPS:
            ref = gathered.at[0, y, pl.ds(group * GROUP, GROUP)]
            copy = pltpu.make_async_remote_copy(
                src_ref=ref,
                dst_ref=ref,
                send_sem=column_line_send.at[group, step - 1],
                recv_sem=second_recv.at[0, group, step - 1],
                device_id={"tiles": along_y(step)},
            )
            copy.start()
            column_lines[group, step] = copy

    for load in load_blocks:
        load.wait()
    partner_copies[CHUNKS].wait_recv()
    their_entries = pltpu.make_async_copy(entry_rows.at[1], entries.at[1], entry_sems.at[1])
    their_entries.start()
    for copy in partner_copies[:CHUNKS]:
        copy.wait_recv()
    own_entries.wait()
    their_entries.wait()

    def product(which, line, index):
        low = 2 * index + (line + which) % 2
        source = (line * RING + low if which == 0 else low * RING + line) * 2 + core
        listed = [blocks[which_list, entries[which_list, 0, source]] for which_list in range(2)]
        return gathered[which, line, index], jnp.concatenate(listed, axis=0)

    total = jnp.zeros((raw.shape[0], 2 * width), jnp.float32)

    def add_line(total, which, line, group):
        pieces = [product(which, line, group * GROUP + i) for i in range(GROUP)]
        left = jnp.concatenate([piece[0] for piece in pieces], axis=1)
        right = jnp.concatenate([piece[1] for piece in pieces], axis=1)
        return total + lax.dot_general(left, right, NT_DIMS, preferred_element_type=jnp.float32)

    for group in range(GROUPS):
        for which in range(2):
            total = add_line(total, which, y if which == 0 else z, group)
        for step in reversed(STEPS):
            for which in range(2):
                ref = gathered.at[which, 0, pl.ds(0, GROUP)]
                pltpu.make_async_copy(ref, ref, second_recv.at[which, group, step - 1]).wait()
                line = ((y if which == 0 else z) + RING - step) % RING
                total = add_line(total, which, line, group)
    for which_list in range(2):
        for group in range(pairs):
            terms[which_list, group] = total[
                group * own_rows : (group + 1) * own_rows,
                which_list * width : (which_list + 1) * width,
            ]

    sums = []
    for step in (2, 1, 3, 0):
        other = (pair + step) % pairs
        for which_list in (1, 0):
            if step == 0 and which_list == 0:
                continue
            number = which_list * pairs + step - 1
            copy = pltpu.make_async_remote_copy(
                src_ref=terms.at[which_list, other],
                dst_ref=arrived.at[number],
                send_sem=sum_send.at[number],
                recv_sem=sum_recv.at[number],
                device_id={"tiles": partner if which_list else tile, "pairs": other},
            )
            copy.start()
            sums.append(copy)
    for copy in partner_copies + list(column_lines.values()):
        copy.wait_send()
    for sent, copy in row_copies + column_copies + list(row_lines.values()):
        pl.when(sent)(copy.wait_send)
    for copy in sums:
        copy.wait_recv()
    near = terms[0, pair]
    for number in range(pairs - 1):
        near += arrived[number]
    far = arrived[pairs - 1]
    for number in range(pairs, 2 * pairs - 1):
        far += arrived[number]
    live = lax.broadcasted_iota(jnp.int32, near.shape, 1) < dims[0]
    out[0] = jnp.where(live, near, 0.0)
    out[1] = jnp.where(live, far, 0.0)
    out[2] = mine_wide[pair]
    for copy in sums:
        copy.wait_send()


def per_device(amplitudes, integrals, block_owner, tile_dims, energy_gap):
    rows, width = amplitudes.shape
    count = integrals.shape[2]
    own_rows = energy_gap.shape[0]
    pairs = rows // own_rows
    dma = pltpu.SemaphoreType.DMA
    out = pl.pallas_call(
        kernel,
        out_shape=jax.ShapeDtypeStruct((3, own_rows, width), jnp.float32),
        in_specs=[pl.BlockSpec(memory_space=pltpu.HBM)] * 4,
        out_specs=pl.BlockSpec(memory_space=pltpu.VMEM),
        scratch_shapes=[
            pltpu.VMEM((1, count), jnp.int32),
            pltpu.SMEM((1,), jnp.int32),
            pltpu.VMEM((rows, width), jnp.bfloat16),
            pltpu.VMEM((2, count + 1, width, width), jnp.bfloat16),
            pltpu.VMEM((rows, width), jnp.bfloat16),
            pltpu.VMEM((pairs, own_rows, width), jnp.float32),
            pltpu.VMEM((2, RING, HALF, rows, width), jnp.bfloat16),
            pltpu.VMEM((2, 8, width), jnp.int32),
            pltpu.SMEM((2, 8, width), jnp.int32),
            pltpu.VMEM((2, pairs, own_rows, width), jnp.float32),
            pltpu.VMEM((2 * pairs - 1, own_rows, width), jnp.float32),
            dma((3 + CHUNKS,)),
            dma((2,)),
            dma((CHUNKS + 1,)),
            dma((CHUNKS + 1,)),
            pltpu.SemaphoreType.REGULAR,
            pltpu.SemaphoreType.REGULAR,
            dma((RING,)),
            dma((RING - 1,)),
            dma((2, GROUPS)),
            dma((GROUPS, RING)),
            dma((GROUPS, RING - 1)),
            dma((2, GROUPS, RING)),
            dma((2 * pairs - 1,)),
            dma((2 * pairs - 1,)),
        ],
        compiler_params=pltpu.CompilerParams(
            collective_id=0, has_side_effects=True, vmem_limit_bytes=62 * 2**20
        ),
        cost_estimate=pl.CostEstimate(
            flops=2 * count * rows * width * width,
            bytes_accessed=2 * count * width * width,
            transcendentals=0,
        ),
    )(block_owner.reshape(1, count), tile_dims, amplitudes, integrals)
    residual = out[0] + out[1]
    return residual, (out[2] - residual / energy_gap).astype(jnp.bfloat16)


def solution(mesh):
    in_specs = (
        P(None, "tiles"),
        P("tiles", "pairs", None, None, None),
        P("tiles", "pairs", None, None),
        P("tiles"),
        P("pairs", "tiles"),
    )
    out_specs = (P("pairs", "tiles"), P("pairs", "tiles"))
    return jax.shard_map(
        per_device, mesh=mesh, in_specs=in_specs, out_specs=out_specs, check_vma=False
    )
```

```python
import jax
import jax.numpy as jnp
from jax import lax
from jax.experimental import pallas as pl
from jax.experimental.pallas import tpu as pltpu
from jax.sharding import PartitionSpec as P

RING = 8
HALF = RING // 2
GROUP = 2
GROUPS = HALF // GROUP
CHUNKS = 4
STEPS = (4, 3, 5, 2, 6, 1, 7)
ROWS = (0, 1, 2, 3, 7, 6, 5, 4)
EARLY, LATE = range(HALF), range(HALF, RING)
NT_DIMS = (((1,), (1,)), ((), ()))


def kernel(
    owners_in,
    dims_in,
    amplitudes,
    integrals,
    out,
    owners,
    dims,
    raw,
    blocks,
    mine,
    mine_wide,
    gathered,
    entry_rows,
    entries,
    terms,
    arrived,
    load_sems,
    entry_sems,
    partner_send,
    partner_recv,
    straight_send,
    row_in,
    column_in,
    late_in,
    late_go,
    row_send,
    column_send,
    first_recv,
    row_line_send,
    column_line_send,
    second_recv,
    sum_send,
    sum_recv,
):
    tile = lax.axis_index("tiles")
    pair = lax.axis_index("pairs")
    pairs = lax.axis_size("pairs")
    core = tile % 2
    z = (tile // 2) % RING
    y = tile // (2 * RING)
    kind = (y + z) % 2
    partner = tile + 1 - 2 * core
    count = blocks.shape[1] - 1
    part = count // CHUNKS

    early = z < HALF

    def in_row(column):
        return (y * RING + column) * 2 + core

    def along_y(step):
        return (((y + step) % RING) * RING + z) * 2 + core

    load_raw = pltpu.make_async_copy(amplitudes, raw, load_sems.at[0])
    load_dims = pltpu.make_async_copy(dims_in, dims, load_sems.at[1])
    load_owners = pltpu.make_async_copy(owners_in, owners, load_sems.at[2])
    load_raw.start()
    load_dims.start()

    barrier = pltpu.get_barrier_semaphore()
    for which in range(2):

        @pl.when(kind == which)
        def _():
            for step in STEPS:
                if (which + step) % 2 == 1:
                    pl.semaphore_signal(barrier, inc=1, device_id={"tiles": along_y(step)})

    for step in range(1, pairs):
        other = (pair + step) % pairs
        pl.semaphore_signal(barrier, inc=1, device_id={"pairs": other})
        pl.semaphore_signal(barrier, inc=1, device_id={"tiles": partner, "pairs": other})
    pl.semaphore_signal(barrier, inc=1, device_id={"tiles": partner})

    @pl.when(early)
    def _():
        for column in LATE:
            pl.semaphore_signal(barrier, inc=1, device_id={"tiles": in_row(column)})
        for column in EARLY:

            @pl.when(jnp.logical_and(z != column, (y + column) % 2 == 0))
            def _():
                pl.semaphore_signal(barrier, inc=1, device_id={"tiles": in_row(column)})

    mate = in_row(z + 1 - 2 * (z % 2))

    @pl.when(jnp.logical_and(kind == 1, jnp.logical_not(early)))
    def _():
        pl.semaphore_signal(barrier, inc=1, device_id={"tiles": mate})

    @pl.when(z == 0)
    def _():
        for step in range(RING):
            for column in range(1, RING):
                if step == 0 and column >= HALF:
                    continue
                other = (((y + step) % RING) * RING + column) * 2 + core

                @pl.when((y + step + column) % 2 == 1)
                def _():
                    pl.semaphore_signal(barrier, inc=1, device_id={"tiles": other})

    load_owners.start()
    load_blocks = []
    for i in range(CHUNKS):
        rows = pl.ds(i * part, part)
        load = pltpu.make_async_copy(
            integrals.at[0, 0, rows], blocks.at[0, rows], load_sems.at[3 + i]
        )
        load.start()
        load_blocks.append(load)
    blocks[0, count] = jnp.zeros(blocks.shape[2:], blocks.dtype)
    blocks[1, count] = jnp.zeros(blocks.shape[2:], blocks.dtype)

    load_dims.wait()
    load_raw.wait()
    columns = lax.broadcasted_iota(jnp.int32, raw.shape, 1)
    masked = jnp.where(columns < dims[0], raw[...].astype(jnp.float32), 0.0)
    mine[...] = masked.astype(jnp.bfloat16)
    own_rows = terms.shape[2]
    for group in range(pairs):
        mine_wide[group] = masked[group * own_rows : (group + 1) * own_rows]
    major = jnp.where(kind == 0, y, z)
    minor = jnp.where(kind == 0, z, y) // 2
    slot = gathered.at[kind, major, minor]
    keep = pltpu.make_async_copy(mine, slot, first_recv.at[kind, minor // GROUP])
    keep.start()

    from_row = jnp.where(early, jnp.where(kind == 0, HALF - 1, 0), HALF + 1 - kind)
    from_column = jnp.where(kind == 0, 0, RING - 1)
    straight = jnp.logical_and(kind == 1, z != 0)
    from_first = jnp.where(straight, jnp.where(early, RING, RING - 1), 0)
    pl.semaphore_wait(barrier, 2 * (pairs - 1) + 1 + from_row + from_column + from_first)

    straight_copies = [
        pltpu.make_async_remote_copy(
            src_ref=mine,
            dst_ref=slot,
            send_sem=straight_send.at[row],
            recv_sem=second_recv.at[1, minor // GROUP, RING - 1 - z],
            device_id={"tiles": row * RING * 2 + core},
        )
        for row in ROWS
    ]

    @pl.when(straight)
    def _():
        for copy in straight_copies:
            copy.start()

    row_copies = []
    for column in range(RING):
        copy = pltpu.make_async_remote_copy(
            src_ref=mine,
            dst_ref=slot,
            send_sem=row_send.at[column],
            recv_sem=first_recv.at[0, minor // GROUP],
            device_id={"tiles": in_row(column)},
        )
        row_copies.append((jnp.logical_and(kind == 0, z != column), copy))
    column_copies = []
    for step in STEPS:
        copy = pltpu.make_async_remote_copy(
            src_ref=mine,
            dst_ref=slot,
            send_sem=column_send.at[step - 1],
            recv_sem=first_recv.at[1, minor // GROUP],
            device_id={"tiles": along_y(step)},
        )
        column_copies.append((kind == 1, copy))
    for column in EARLY:
        pl.when(row_copies[column][0])(row_copies[column][1].start)

    @pl.when(kind == 1)
    def _():
        pl.semaphore_signal(column_in, inc=1, device_id={"tiles": along_y(1)})
        for _, copy in column_copies:
            copy.start()

    @pl.when(jnp.logical_and(kind == 0, early))
    def _():
        pl.semaphore_signal(row_in, inc=1, device_id={"tiles": mate})

    @pl.when(jnp.logical_and(kind == 0, jnp.logical_not(early)))
    def _():
        for column in EARLY:
            pl.semaphore_signal(late_in, inc=1, device_id={"tiles": in_row(column)})

    partner_copies = []
    for i in range(CHUNKS):
        rows = pl.ds(i * part, part)
        copy = pltpu.make_async_remote_copy(
            src_ref=integrals.at[0, 0, rows],
            dst_ref=blocks.at[1, rows],
            send_sem=partner_send.at[i],
            recv_sem=partner_recv.at[i],
            device_id={"tiles": partner},
        )
        copy.start()
        partner_copies.append(copy)

    load_owners.wait()
    width = raw.shape[1]
    row = jnp.broadcast_to(owners[...], (width, count))
    row = jnp.concatenate([row, jnp.full((width, width - count), -1, jnp.int32)], axis=1)
    named = row.T == lax.broadcasted_iota(jnp.int32, (width, width), 1)
    places = lax.broadcasted_iota(jnp.int32, (width, width), 0)
    place = jnp.min(jnp.where(named, places, count), axis=0, keepdims=True)
    entry_rows[0] = jnp.broadcast_to(place, entry_rows.shape[1:])
    copy = pltpu.make_async_remote_copy(
        src_ref=entry_rows.at[0],
        dst_ref=entry_rows.at[1],
        send_sem=partner_send.at[CHUNKS],
        recv_sem=partner_recv.at[CHUNKS],
        device_id={"tiles": partner},
    )
    copy.start()
    partner_copies.append(copy)
    own_entries = pltpu.make_async_copy(entry_rows.at[0], entries.at[0], entry_sems.at[0])
    own_entries.start()

    def wait_first(which, group):
        ref = gathered.at[which, 0, pl.ds(0, GROUP)]
        pltpu.make_async_copy(ref, ref, first_recv.at[which, group]).wait()

    row_lines = {}
    for group in range(GROUPS):
        for column in range(1, RING):
            ref = gathered.at[1, z, pl.ds(group * GROUP, GROUP)]
            copy = pltpu.make_async_remote_copy(
                src_ref=ref,
                dst_ref=ref,
                send_sem=row_line_send.at[group, column],
                recv_sem=second_recv.at[1, group, (column + RING - 1 - z) % RING],
                device_id={"tiles": in_row(column)},
            )
            row_lines[group, column] = (z != column, copy)
    column_lines = {}
    for group in range(GROUPS):
        for row in ROWS:
            ref = gathered.at[0, y, pl.ds(group * GROUP, GROUP)]
            copy = pltpu.make_async_remote_copy(
                src_ref=ref,
                dst_ref=ref,
                send_sem=column_line_send.at[group, row],
                recv_sem=second_recv.at[0, group, (row + RING - 1 - y) % RING],
                device_id={"tiles": (row * RING + z) * 2 + core},
            )
            column_lines[group, row] = (y != row, copy)

    def send_column_lines(groups):
        for group in groups:
            wait_first(0, group)
            for row in ROWS:
                pl.when(column_lines[group, row][0])(column_lines[group, row][1].start)

    def send_early_lines():
        for group in range(GROUPS):
            wait_first(1, group)
            for column in EARLY[1:]:
                pl.when(row_lines[group, column][0])(row_lines[group, column][1].start)

    @pl.when(early)
    def _():
        @pl.when(kind == 1)
        def _():
            pl.semaphore_wait(row_in, 1)

        send_early_lines()

        @pl.when(kind == 0)
        def _():
            pl.semaphore_wait(column_in, 1)

        send_column_lines(range(GROUPS // 2))
        pl.semaphore_wait(late_in, HALF // 2)

    @pl.when(z == 0)
    def _():
        for column in LATE:
            pl.semaphore_signal(late_go, inc=1, device_id={"tiles": in_row(column)})

    @pl.when(jnp.logical_not(early))
    def _():
        pl.semaphore_wait(late_go, 1)

    for column in (6, 5, 7, 4):
        pl.when(row_copies[column][0])(row_copies[column][1].start)
    pl.when(jnp.logical_not(early))(send_early_lines)
    @pl.when(jnp.logical_not(early))
    def _():
        @pl.when(kind == 0)
        def _():
            pl.semaphore_wait(column_in, 1)

        send_column_lines(range(GROUPS // 2))

    send_column_lines(range(GROUPS // 2, GROUPS))

    for group in range(GROUPS):
        for column in (6, 5, 7, 4):
            pl.when(row_lines[group, column][0])(row_lines[group, column][1].start)
    for load in load_blocks:
        load.wait()
    partner_copies[CHUNKS].wait_recv()
    their_entries = pltpu.make_async_copy(entry_rows.at[1], entries.at[1], entry_sems.at[1])
    their_entries.start()
    for copy in partner_copies[:CHUNKS]:
        copy.wait_recv()
    own_entries.wait()
    their_entries.wait()

    def product(which, line, index):
        low = 2 * index + (line + which) % 2
        source = (line * RING + low if which == 0 else low * RING + line) * 2 + core
        listed = [blocks[which_list, entries[which_list, 0, source]] for which_list in range(2)]
        return gathered[which, line, index], jnp.concatenate(listed, axis=0)

    total = jnp.zeros((raw.shape[0], 2 * width), jnp.float32)

    def add_line(total, which, line, group):
        pieces = [product(which, line, group * GROUP + i) for i in range(GROUP)]
        left = jnp.concatenate([piece[0] for piece in pieces], axis=1)
        right = jnp.concatenate([piece[1] for piece in pieces], axis=1)
        return total + lax.dot_general(left, right, NT_DIMS, preferred_element_type=jnp.float32)

    for group in range(GROUPS):
        for which in range(2):
            total = add_line(total, which, y if which == 0 else z, group)
        for step in reversed(STEPS):
            for which in range(2):
                ref = gathered.at[which, 0, pl.ds(0, GROUP)]
                pltpu.make_async_copy(ref, ref, second_recv.at[which, group, step - 1]).wait()
                line = ((y if which == 0 else z) + RING - step) % RING
                total = add_line(total, which, line, group)
    for which_list in range(2):
        for group in range(pairs):
            terms[which_list, group] = total[
                group * own_rows : (group + 1) * own_rows,
                which_list * width : (which_list + 1) * width,
            ]

    sums = []
    for step in (2, 1, 3, 0):
        other = (pair + step) % pairs
        for which_list in (1, 0):
            if step == 0 and which_list == 0:
                continue
            number = which_list * pairs + step - 1
            copy = pltpu.make_async_remote_copy(
                src_ref=terms.at[which_list, other],
                dst_ref=arrived.at[number],
                send_sem=sum_send.at[number],
                recv_sem=sum_recv.at[number],
                device_id={"tiles": partner if which_list else tile, "pairs": other},
            )
            copy.start()
            sums.append(copy)
    for copy in partner_copies:
        copy.wait_send()
    lines = list(row_lines.values()) + list(column_lines.values())
    for sent, copy in row_copies + column_copies + lines:
        pl.when(sent)(copy.wait_send)

    @pl.when(straight)
    def _():
        for copy in straight_copies:
            copy.wait_send()

    for copy in sums:
        copy.wait_recv()
    near = terms[0, pair]
    for number in range(pairs - 1):
        near += arrived[number]
    far = arrived[pairs - 1]
    for number in range(pairs, 2 * pairs - 1):
        far += arrived[number]
    live = lax.broadcasted_iota(jnp.int32, near.shape, 1) < dims[0]
    out[0] = jnp.where(live, near, 0.0)
    out[1] = jnp.where(live, far, 0.0)
    out[2] = mine_wide[pair]
    for copy in sums:
        copy.wait_send()


def per_device(amplitudes, integrals, block_owner, tile_dims, energy_gap):
    rows, width = amplitudes.shape
    count = integrals.shape[2]
    own_rows = energy_gap.shape[0]
    pairs = rows // own_rows
    dma = pltpu.SemaphoreType.DMA
    out = pl.pallas_call(
        kernel,
        out_shape=jax.ShapeDtypeStruct((3, own_rows, width), jnp.float32),
        in_specs=[pl.BlockSpec(memory_space=pltpu.HBM)] * 4,
        out_specs=pl.BlockSpec(memory_space=pltpu.VMEM),
        scratch_shapes=[
            pltpu.VMEM((1, count), jnp.int32),
            pltpu.SMEM((1,), jnp.int32),
            pltpu.VMEM((rows, width), jnp.bfloat16),
            pltpu.VMEM((2, count + 1, width, width), jnp.bfloat16),
            pltpu.VMEM((rows, width), jnp.bfloat16),
            pltpu.VMEM((pairs, own_rows, width), jnp.float32),
            pltpu.VMEM((2, RING, HALF, rows, width), jnp.bfloat16),
            pltpu.VMEM((2, 8, width), jnp.int32),
            pltpu.SMEM((2, 8, width), jnp.int32),
            pltpu.VMEM((2, pairs, own_rows, width), jnp.float32),
            pltpu.VMEM((2 * pairs - 1, own_rows, width), jnp.float32),
            dma((3 + CHUNKS,)),
            dma((2,)),
            dma((CHUNKS + 1,)),
            dma((CHUNKS + 1,)),
            dma((RING,)),
            pltpu.SemaphoreType.REGULAR,
            pltpu.SemaphoreType.REGULAR,
            pltpu.SemaphoreType.REGULAR,
            pltpu.SemaphoreType.REGULAR,
            dma((RING,)),
            dma((RING - 1,)),
            dma((2, GROUPS)),
            dma((GROUPS, RING)),
            dma((GROUPS, RING)),
            dma((2, GROUPS, RING)),
            dma((2 * pairs - 1,)),
            dma((2 * pairs - 1,)),
        ],
        compiler_params=pltpu.CompilerParams(
            collective_id=0, has_side_effects=True, vmem_limit_bytes=62 * 2**20
        ),
        cost_estimate=pl.CostEstimate(
            flops=2 * count * rows * width * width,
            bytes_accessed=2 * count * width * width,
            transcendentals=0,
        ),
    )(block_owner.reshape(1, count), tile_dims, amplitudes, integrals)
    residual = out[0] + out[1]
    return residual, (out[2] - residual / energy_gap).astype(jnp.bfloat16)


def solution(mesh):
    in_specs = (
        P(None, "tiles"),
        P("tiles", "pairs", None, None, None),
        P("tiles", "pairs", None, None),
        P("tiles"),
        P("pairs", "tiles"),
    )
    out_specs = (P("pairs", "tiles"), P("pairs", "tiles"))
    return jax.shard_map(
        per_device, mesh=mesh, in_specs=in_specs, out_specs=out_specs, check_vma=False
    )
```

```python
import jax
import jax.numpy as jnp
from jax import lax
from jax.experimental import pallas as pl
from jax.experimental.pallas import tpu as pltpu
from jax.sharding import PartitionSpec as P

RING = 8
HALF = RING // 2
GROUP = 2
GROUPS = HALF // GROUP
CHUNKS = 4
STEPS = (4, 3, 5, 2, 6, 1, 7)
ROWS = (0, 1, 2, 3, 7, 6, 5, 4)
EARLY, LATE = range(HALF), range(HALF, RING)
NT_DIMS = (((1,), (1,)), ((), ()))


def kernel(
    owners_in,
    dims_in,
    amplitudes,
    integrals,
    out,
    owners,
    dims,
    raw,
    blocks,
    mine,
    mine_wide,
    gathered,
    entry_rows,
    entries,
    terms,
    arrived,
    load_sems,
    entry_sems,
    partner_send,
    partner_recv,
    straight_send,
    row_in,
    column_in,
    late_in,
    late_go,
    row_send,
    column_send,
    first_recv,
    row_line_send,
    column_line_send,
    second_recv,
    sum_send,
    sum_recv,
):
    tile = lax.axis_index("tiles")
    pair = lax.axis_index("pairs")
    pairs = lax.axis_size("pairs")
    core = tile % 2
    z = (tile // 2) % RING
    y = tile // (2 * RING)
    kind = (y + z) % 2
    partner = tile + 1 - 2 * core
    count = blocks.shape[1] - 1
    part = count // CHUNKS

    early = z < HALF

    def in_row(column):
        return (y * RING + column) * 2 + core

    def along_y(step):
        return (((y + step) % RING) * RING + z) * 2 + core

    load_raw = pltpu.make_async_copy(amplitudes, raw, load_sems.at[0])
    load_dims = pltpu.make_async_copy(dims_in, dims, load_sems.at[1])
    load_owners = pltpu.make_async_copy(owners_in, owners, load_sems.at[2])
    load_raw.start()
    load_dims.start()

    barrier = pltpu.get_barrier_semaphore()
    for which in range(2):

        @pl.when(kind == which)
        def _():
            for step in STEPS:
                if (which + step) % 2 == 1:
                    pl.semaphore_signal(barrier, inc=1, device_id={"tiles": along_y(step)})

    for step in range(1, pairs):
        other = (pair + step) % pairs
        pl.semaphore_signal(barrier, inc=1, device_id={"pairs": other})
        pl.semaphore_signal(barrier, inc=1, device_id={"tiles": partner, "pairs": other})
    pl.semaphore_signal(barrier, inc=1, device_id={"tiles": partner})

    @pl.when(early)
    def _():
        for column in LATE:
            pl.semaphore_signal(barrier, inc=1, device_id={"tiles": in_row(column)})
        for column in EARLY:

            @pl.when(jnp.logical_and(z != column, (y + column) % 2 == 0))
            def _():
                pl.semaphore_signal(barrier, inc=1, device_id={"tiles": in_row(column)})

    mate = in_row(z + 1 - 2 * (z % 2))

    @pl.when(jnp.logical_and(kind == 1, jnp.logical_not(early)))
    def _():
        pl.semaphore_signal(barrier, inc=1, device_id={"tiles": mate})

    @pl.when(z == 0)
    def _():
        for step in range(RING):
            for column in range(1, RING):
                if step == 0 and column >= HALF:
                    continue
                other = (((y + step) % RING) * RING + column) * 2 + core

                @pl.when((y + step + column) % 2 == 1)
                def _():
                    pl.semaphore_signal(barrier, inc=1, device_id={"tiles": other})

    load_owners.start()
    load_blocks = []
    for i in range(CHUNKS):
        rows = pl.ds(i * part, part)
        load = pltpu.make_async_copy(
            integrals.at[0, 0, rows], blocks.at[0, rows], load_sems.at[3 + i]
        )
        load.start()
        load_blocks.append(load)
    blocks[0, count] = jnp.zeros(blocks.shape[2:], blocks.dtype)
    blocks[1, count] = jnp.zeros(blocks.shape[2:], blocks.dtype)

    load_dims.wait()
    load_raw.wait()
    columns = lax.broadcasted_iota(jnp.int32, raw.shape, 1)
    masked = jnp.where(columns < dims[0], raw[...].astype(jnp.float32), 0.0)
    mine[...] = masked.astype(jnp.bfloat16)
    own_rows = terms.shape[2]
    for group in range(pairs):
        mine_wide[group] = masked[group * own_rows : (group + 1) * own_rows]
    major = jnp.where(kind == 0, y, z)
    minor = jnp.where(kind == 0, z, y) // 2
    slot = gathered.at[kind, major, minor]
    keep = pltpu.make_async_copy(mine, slot, first_recv.at[kind, minor // GROUP])
    keep.start()

    from_row = jnp.where(early, jnp.where(kind == 0, HALF - 1, 0), HALF + 1 - kind)
    from_column = jnp.where(kind == 0, 0, RING - 1)
    straight = jnp.logical_and(kind == 1, z != 0)
    from_first = jnp.where(straight, jnp.where(early, RING, RING - 1), 0)
    pl.semaphore_wait(barrier, 2 * (pairs - 1) + 1 + from_row + from_column + from_first)

    straight_copies = [
        pltpu.make_async_remote_copy(
            src_ref=mine,
            dst_ref=slot,
            send_sem=straight_send.at[row],
            recv_sem=second_recv.at[1, minor // GROUP, RING - 1 - z],
            device_id={"tiles": row * RING * 2 + core},
        )
        for row in ROWS
    ]

    @pl.when(straight)
    def _():
        for copy in straight_copies:
            copy.start()

    row_copies = []
    for column in range(RING):
        copy = pltpu.make_async_remote_copy(
            src_ref=mine,
            dst_ref=slot,
            send_sem=row_send.at[column],
            recv_sem=first_recv.at[0, minor // GROUP],
            device_id={"tiles": in_row(column)},
        )
        row_copies.append((jnp.logical_and(kind == 0, z != column), copy))
    column_copies = []
    for step in STEPS:
        copy = pltpu.make_async_remote_copy(
            src_ref=mine,
            dst_ref=slot,
            send_sem=column_send.at[step - 1],
            recv_sem=first_recv.at[1, minor // GROUP],
            device_id={"tiles": along_y(step)},
        )
        column_copies.append((kind == 1, copy))
    for column in EARLY:
        pl.when(row_copies[column][0])(row_copies[column][1].start)

    @pl.when(kind == 1)
    def _():
        pl.semaphore_signal(column_in, inc=1, device_id={"tiles": along_y(1)})
        for _, copy in column_copies:
            copy.start()

    @pl.when(jnp.logical_and(kind == 0, early))
    def _():
        pl.semaphore_signal(row_in, inc=1, device_id={"tiles": mate})

    @pl.when(jnp.logical_and(kind == 0, jnp.logical_not(early)))
    def _():
        for column in EARLY:
            pl.semaphore_signal(late_in, inc=1, device_id={"tiles": in_row(column)})

    partner_copies = []
    for i in range(CHUNKS):
        rows = pl.ds(i * part, part)
        copy = pltpu.make_async_remote_copy(
            src_ref=integrals.at[0, 0, rows],
            dst_ref=blocks.at[1, rows],
            send_sem=partner_send.at[i],
            recv_sem=partner_recv.at[i],
            device_id={"tiles": partner},
        )
        copy.start()
        partner_copies.append(copy)

    load_owners.wait()
    width = raw.shape[1]
    row = jnp.broadcast_to(owners[...], (width, count))
    row = jnp.concatenate([row, jnp.full((width, width - count), -1, jnp.int32)], axis=1)
    named = row.T == lax.broadcasted_iota(jnp.int32, (width, width), 1)
    places = lax.broadcasted_iota(jnp.int32, (width, width), 0)
    place = jnp.min(jnp.where(named, places, count), axis=0, keepdims=True)
    entry_rows[0] = jnp.broadcast_to(place, entry_rows.shape[1:])
    copy = pltpu.make_async_remote_copy(
        src_ref=entry_rows.at[0],
        dst_ref=entry_rows.at[1],
        send_sem=partner_send.at[CHUNKS],
        recv_sem=partner_recv.at[CHUNKS],
        device_id={"tiles": partner},
    )
    copy.start()
    partner_copies.append(copy)
    own_entries = pltpu.make_async_copy(entry_rows.at[0], entries.at[0], entry_sems.at[0])
    own_entries.start()

    def wait_first(which, group):
        ref = gathered.at[which, 0, pl.ds(0, GROUP)]
        pltpu.make_async_copy(ref, ref, first_recv.at[which, group]).wait()

    row_lines = {}
    for group in range(GROUPS):
        for column in range(1, RING):
            ref = gathered.at[1, z, pl.ds(group * GROUP, GROUP)]
            copy = pltpu.make_async_remote_copy(
                src_ref=ref,
                dst_ref=ref,
                send_sem=row_line_send.at[group, column],
                recv_sem=second_recv.at[1, group, (column + RING - 1 - z) % RING],
                device_id={"tiles": in_row(column)},
            )
            row_lines[group, column] = (z != column, copy)
    column_lines = {}
    for group in range(GROUPS):
        for row in ROWS:
            ref = gathered.at[0, y, pl.ds(group * GROUP, GROUP)]
            copy = pltpu.make_async_remote_copy(
                src_ref=ref,
                dst_ref=ref,
                send_sem=column_line_send.at[group, row],
                recv_sem=second_recv.at[0, group, (row + RING - 1 - y) % RING],
                device_id={"tiles": (row * RING + z) * 2 + core},
            )
            column_lines[group, row] = (y != row, copy)

    def send_column_lines(groups):
        for group in groups:
            wait_first(0, group)
            for row in ROWS:
                pl.when(column_lines[group, row][0])(column_lines[group, row][1].start)

    def send_early_lines():
        for group in range(GROUPS):
            wait_first(1, group)
            for column in EARLY[1:]:
                pl.when(row_lines[group, column][0])(row_lines[group, column][1].start)

    @pl.when(early)
    def _():
        @pl.when(kind == 0)
        def _():
            pl.semaphore_wait(column_in, 1)

        send_column_lines(range(GROUPS // 2))

        @pl.when(kind == 1)
        def _():
            pl.semaphore_wait(row_in, 1)

        send_early_lines()
        pl.semaphore_wait(late_in, HALF // 2)

    @pl.when(z == 0)
    def _():
        for column in LATE:
            pl.semaphore_signal(late_go, inc=1, device_id={"tiles": in_row(column)})

    @pl.when(jnp.logical_not(early))
    def _():
        pl.semaphore_wait(late_go, 1)

    for column in (6, 5, 7, 4):
        pl.when(row_copies[column][0])(row_copies[column][1].start)
    pl.when(jnp.logical_not(early))(send_early_lines)
    @pl.when(jnp.logical_not(early))
    def _():
        @pl.when(kind == 0)
        def _():
            pl.semaphore_wait(column_in, 1)

        send_column_lines(range(GROUPS // 2))

    send_column_lines(range(GROUPS // 2, GROUPS))

    for group in range(GROUPS):
        for column in (6, 5, 7, 4):
            pl.when(row_lines[group, column][0])(row_lines[group, column][1].start)
    for load in load_blocks:
        load.wait()
    partner_copies[CHUNKS].wait_recv()
    their_entries = pltpu.make_async_copy(entry_rows.at[1], entries.at[1], entry_sems.at[1])
    their_entries.start()
    for copy in partner_copies[:CHUNKS]:
        copy.wait_recv()
    own_entries.wait()
    their_entries.wait()

    def product(which, line, index):
        low = 2 * index + (line + which) % 2
        source = (line * RING + low if which == 0 else low * RING + line) * 2 + core
        listed = [blocks[which_list, entries[which_list, 0, source]] for which_list in range(2)]
        return gathered[which, line, index], jnp.concatenate(listed, axis=0)

    total = jnp.zeros((raw.shape[0], 2 * width), jnp.float32)

    def add_line(total, which, line, group):
        pieces = [product(which, line, group * GROUP + i) for i in range(GROUP)]
        left = jnp.concatenate([piece[0] for piece in pieces], axis=1)
        right = jnp.concatenate([piece[1] for piece in pieces], axis=1)
        return total + lax.dot_general(left, right, NT_DIMS, preferred_element_type=jnp.float32)

    for group in range(GROUPS):
        for which in range(2):
            total = add_line(total, which, y if which == 0 else z, group)
        for step in reversed(STEPS):
            for which in range(2):
                ref = gathered.at[which, 0, pl.ds(0, GROUP)]
                pltpu.make_async_copy(ref, ref, second_recv.at[which, group, step - 1]).wait()
                line = ((y if which == 0 else z) + RING - step) % RING
                total = add_line(total, which, line, group)
    for which_list in range(2):
        for group in range(pairs):
            terms[which_list, group] = total[
                group * own_rows : (group + 1) * own_rows,
                which_list * width : (which_list + 1) * width,
            ]

    sums = []
    for step in (2, 1, 3, 0):
        other = (pair + step) % pairs
        for which_list in (1, 0):
            if step == 0 and which_list == 0:
                continue
            number = which_list * pairs + step - 1
            copy = pltpu.make_async_remote_copy(
                src_ref=terms.at[which_list, other],
                dst_ref=arrived.at[number],
                send_sem=sum_send.at[number],
                recv_sem=sum_recv.at[number],
                device_id={"tiles": partner if which_list else tile, "pairs": other},
            )
            copy.start()
            sums.append(copy)
    for copy in partner_copies:
        copy.wait_send()
    lines = list(row_lines.values()) + list(column_lines.values())
    for sent, copy in row_copies + column_copies + lines:
        pl.when(sent)(copy.wait_send)

    @pl.when(straight)
    def _():
        for copy in straight_copies:
            copy.wait_send()

    for copy in sums:
        copy.wait_recv()
    near = terms[0, pair]
    for number in range(pairs - 1):
        near += arrived[number]
    far = arrived[pairs - 1]
    for number in range(pairs, 2 * pairs - 1):
        far += arrived[number]
    live = lax.broadcasted_iota(jnp.int32, near.shape, 1) < dims[0]
    out[0] = jnp.where(live, near, 0.0)
    out[1] = jnp.where(live, far, 0.0)
    out[2] = mine_wide[pair]
    for copy in sums:
        copy.wait_send()


def per_device(amplitudes, integrals, block_owner, tile_dims, energy_gap):
    rows, width = amplitudes.shape
    count = integrals.shape[2]
    own_rows = energy_gap.shape[0]
    pairs = rows // own_rows
    dma = pltpu.SemaphoreType.DMA
    out = pl.pallas_call(
        kernel,
        out_shape=jax.ShapeDtypeStruct((3, own_rows, width), jnp.float32),
        in_specs=[pl.BlockSpec(memory_space=pltpu.HBM)] * 4,
        out_specs=pl.BlockSpec(memory_space=pltpu.VMEM),
        scratch_shapes=[
            pltpu.VMEM((1, count), jnp.int32),
            pltpu.SMEM((1,), jnp.int32),
            pltpu.VMEM((rows, width), jnp.bfloat16),
            pltpu.VMEM((2, count + 1, width, width), jnp.bfloat16),
            pltpu.VMEM((rows, width), jnp.bfloat16),
            pltpu.VMEM((pairs, own_rows, width), jnp.float32),
            pltpu.VMEM((2, RING, HALF, rows, width), jnp.bfloat16),
            pltpu.VMEM((2, 8, width), jnp.int32),
            pltpu.SMEM((2, 8, width), jnp.int32),
            pltpu.VMEM((2, pairs, own_rows, width), jnp.float32),
            pltpu.VMEM((2 * pairs - 1, own_rows, width), jnp.float32),
            dma((3 + CHUNKS,)),
            dma((2,)),
            dma((CHUNKS + 1,)),
            dma((CHUNKS + 1,)),
            dma((RING,)),
            pltpu.SemaphoreType.REGULAR,
            pltpu.SemaphoreType.REGULAR,
            pltpu.SemaphoreType.REGULAR,
            pltpu.SemaphoreType.REGULAR,
            dma((RING,)),
            dma((RING - 1,)),
            dma((2, GROUPS)),
            dma((GROUPS, RING)),
            dma((GROUPS, RING)),
            dma((2, GROUPS, RING)),
            dma((2 * pairs - 1,)),
            dma((2 * pairs - 1,)),
        ],
        compiler_params=pltpu.CompilerParams(
            collective_id=0, has_side_effects=True, vmem_limit_bytes=62 * 2**20
        ),
        cost_estimate=pl.CostEstimate(
            flops=2 * count * rows * width * width,
            bytes_accessed=2 * count * width * width,
            transcendentals=0,
        ),
    )(block_owner.reshape(1, count), tile_dims, amplitudes, integrals)
    residual = out[0] + out[1]
    return residual, (out[2] - residual / energy_gap).astype(jnp.bfloat16)


def solution(mesh):
    in_specs = (
        P(None, "tiles"),
        P("tiles", "pairs", None, None, None),
        P("tiles", "pairs", None, None),
        P("tiles"),
        P("pairs", "tiles"),
    )
    out_specs = (P("pairs", "tiles"), P("pairs", "tiles"))
    return jax.shard_map(
        per_device, mesh=mesh, in_specs=in_specs, out_specs=out_specs, check_vma=False
    )
```
